32 devices in a mesh: section: 8 (over z, x), dp: 4 (over y, core).
Axes of the slice: x: 2, y: 2, z: 4, core: 2. Of those that a mesh axis runs over, the one named last changes fastest.
Arguments:
- section_inputs: bfloat16 [8, 768, 1152], P('section'), may hold values from -6 to 6
- mirror_held: bfloat16 [8, 768, 1152], P('section'), may hold values from -6 to 6
- section_cotangents: bfloat16 [8, 768, 1152], P('section'), may hold values from -6 to 6
- next_batch: bfloat16 [768, 1152], replicated, may hold values from -6 to 6
- loss_cotangent: bfloat16 [768, 1152], replicated, may hold values from -6 to 6
- join_weights: bfloat16 [8, 1152, 1152], P('section'), may hold values from -0.125 to 0.125
Outputs:
- section_outputs: bfloat16 [32, 2, 768, 1152], P(('dp', 'section')), parts along dimension 0
- section_gradients: bfloat16 [32, 2, 768, 1152], P(('dp', 'section')), parts along dimension 0
- mirror_arrivals: bfloat16 [32, 768, 1152], P(('dp', 'section')), parts along dimension 0
The draws below stay inside these ranges and needn't reach their ends.
There are 4 independent parts, one for each index of `dp`. The reference program is written for one: setup_inputs(seed, part) draws one part's arguments, and reference() takes and returns one part's arrays. A program takes and returns all parts, laid end to end along the dimension named above; an argument that names none is the same for every part. Nothing has to cross between parts.
All inputs are finite; a program needn't handle non-finite values.
Results may differ from the reference program's by a relative error of at most 0.001.
Values may be sent and summed in bfloat16 or wider, within the bound.
A program may use at most 128 MiB of HBM per device.

```python
import jax
import jax.numpy as jnp

D = 1152
ROWS = 768
SECTIONS = 8


def steps_of(rng, extent, shards, smallest, largest):
    def one(position, shards_of):
        steps = jax.random.uniform(jax.random.fold_in(jax.random.fold_in(rng, 6), position), (shards_of,), jnp.float32, smallest / len(shards), largest / len(shards))
        return jnp.repeat(jnp.exp(steps), extent[position] // shards_of).reshape((-1,) + (1,) * (len(extent) - position - 1))

    loudness = one(*shards[0])
    for cut in shards[1:]:
        loudness = loudness * one(*cut)
    return loudness


def gaussian(rng, dims, deviation, most, cuts=(), kind=jnp.bfloat16):
    drawn = deviation * jax.random.normal(rng, dims, jnp.float32)
    if cuts:
        drawn = drawn * steps_of(rng, dims, cuts, -0.22, 0.18)
    return jnp.clip(drawn, -most, most).astype(kind)


def setup_inputs(seed: int = 0, part: int = 0) -> dict:
    key_of = jax.random.split(jax.random.key(seed), 7)
    section_inputs = gaussian(key_of[0], (SECTIONS, ROWS, D), 1.0, 6.0, ((0, 8),))
    mirror_held = gaussian(key_of[1], (SECTIONS, ROWS, D), 1.0, 6.0, ((0, 8),))
    section_cotangents = gaussian(key_of[2], (SECTIONS, ROWS, D), 1.0, 6.0, ((0, 8),))
    next_batch = gaussian(key_of[3], (ROWS, D), 1.0, 6.0)
    loss_cotangent = gaussian(key_of[4], (ROWS, D), 1.0, 6.0)
    join_weights = gaussian(key_of[5], (SECTIONS, D, D), (2 * D) ** -0.5, 0.125, ((0, 8),))
    return dict(section_inputs=section_inputs, mirror_held=mirror_held, section_cotangents=section_cotangents, next_batch=next_batch, loss_cotangent=loss_cotangent, join_weights=join_weights)


def slot_tables(count):
    slots = jnp.arange(count, dtype=jnp.int32)
    even = slots % 2 == 0
    partner = slots + 1 - 2 * (slots % 2)
    before = jnp.where(even, slots - 2, jnp.where(slots == count - 1, count - 2, slots + 2))
    after = jnp.where(even, jnp.where(slots == count - 2, count - 1, slots + 2), slots - 2)
    before = jnp.clip(before, 0, count - 1).astype(jnp.int32)
    after = jnp.clip(after, 0, count - 1).astype(jnp.int32)
    return slots, even[:, None, None], partner.astype(jnp.int32), before, after


def forward_tick(arriving, pending, join_weights, even, partner):
    product = jnp.einsum("srd,sde->sre", arriving.astype(jnp.float32), join_weights.astype(jnp.float32))
    projected = product.astype(jnp.bfloat16)
    joined = (product + pending.astype(jnp.float32)).astype(jnp.bfloat16)
    leaving = jnp.where(even, arriving, joined)
    return leaving, projected[partner]


def backward_tick(cotangent, returned, join_weights, even, partner):
    operand = jnp.where(even, returned, cotangent)
    product = jnp.einsum("sre,sde->srd", operand.astype(jnp.float32), join_weights.astype(jnp.float32))
    grad = jnp.where(even, cotangent.astype(jnp.float32) + product, product).astype(jnp.bfloat16)
    return grad, cotangent[partner]


def reference(section_inputs, mirror_held, section_cotangents, next_batch, loss_cotangent, join_weights):
    count = section_inputs.shape[0]
    slots, even, partner, before, after = slot_tables(count)
    first_out, skips_one = forward_tick(section_inputs, mirror_held, join_weights, even, partner)
    first_grad, returns_one = backward_tick(section_cotangents, mirror_held, join_weights, even, partner)
    second_in = jnp.where((slots == 0)[:, None, None], next_batch[None], first_out[before])
    second_out, skips_two = forward_tick(second_in, skips_one, join_weights, even, partner)
    second_cot = jnp.where((slots == 1)[:, None, None], loss_cotangent[None], first_grad[after])
    second_grad, returns_two = backward_tick(second_cot, returns_one, join_weights, even, partner)
    section_outputs = jnp.stack([first_out, second_out], axis=1)
    section_gradients = jnp.stack([first_grad, second_grad], axis=1)
    mirror_arrivals = jnp.where(even, returns_two, skips_two)
    return section_outputs, section_gradients, mirror_arrivals
```

```python
import functools

import jax
import jax.numpy as jnp
from jax import lax
from jax.experimental import pallas as pl
from jax.experimental.pallas import tpu as pltpu
from jax.sharding import PartitionSpec as P

MESH = pl.DeviceIdType.MESH
CHUNKS = 2


def message_ids():
    ids = {}
    for kind in ("up", "down", "x1", "x2", "core_up", "fc", "fy", "ff", "ac", "ay", "af"):
        for i in range(CHUNKS):
            ids[kind, i] = len(ids)
    for kind in ("up_rest", "core_rest"):
        ids[kind] = len(ids)
    return ids


IDS = message_ids()


def kernel(
    count,
    a_hbm, h_hbm, g_hbm, nb_hbm, lc_hbm, w_hbm,
    out_hbm, grad_hbm, arr_hbm,
    a_v, h_v, g_v, w_v, uin, din, x1, fin, arr, y1, dx1, dx2, s1, s2,
    in_sem, out_sem, send_sem, recv_sem,
):
    rows, _ = a_v.shape
    half, quarter = rows // 2, rows // 4
    chunk = quarter // CHUNKS
    p = lax.axis_index("section")
    d = lax.axis_index("dp")
    mirror = p + 1 - 2 * (p % 2)
    core_peer = d + 1 - 2 * (d % 2)
    y_peer = d + 2 - 4 * ((d // 2) % 2)
    core, yy = d % 2, (d // 2) % 2
    is_even = p % 2 == 0
    is_odd = p % 2 == 1
    has_up = p + 2 < count
    is_top = p + 2 >= count
    has_down = p >= 2
    is_bottom = p < 2
    up = jnp.where(has_up, p + 2, p)
    down = jnp.where(has_down, p - 2, p)

    own = core * half + yy * quarter
    rest = core * half + (1 - yy) * quarter
    across = (1 - core) * half
    y_own = rest

    def rows_at(start, size):
        return pl.ds(pl.multiple_of(start, 16), size)

    def copy(src, dst, ks, kr, section, dp):
        return pltpu.make_async_remote_copy(
            src_ref=src, dst_ref=dst, send_sem=send_sem.at[ks], recv_sem=recv_sem.at[kr],
            device_id=(section, dp), device_id_type=MESH,
        )

    def landed(dst, key):
        k = IDS[key]
        copy(dst, dst, k, k, mirror, d).wait_recv()

    def sent(src, key):
        k = IDS[key]
        copy(src, src, k, k, mirror, d).wait_send()

    loads = [
        pltpu.make_async_copy(src, dst, in_sem.at[i])
        for i, (src, dst) in enumerate(
            ((w_hbm.at[0], w_v), (a_hbm.at[0], a_v), (g_hbm.at[0], g_v), (h_hbm.at[0], h_v))
        )
    ]
    w_load, a_load, g_load, h_load = loads
    for load in loads:
        load.start()
    nb_load = pltpu.make_async_copy(nb_hbm, uin, in_sem.at[4])
    lc_load = pltpu.make_async_copy(lc_hbm, uin, in_sem.at[4])

    @pl.when(p == 0)
    def _():
        nb_load.start()

    @pl.when(p == 1)
    def _():
        lc_load.start()

    barrier = pltpu.get_barrier_semaphore()
    for peer in ((mirror, d), (p, core_peer), (p, y_peer)):
        pl.semaphore_signal(barrier, inc=1, device_id=peer, device_id_type=MESH)

    @pl.when(has_up)
    def _():
        pl.semaphore_signal(barrier, inc=1, device_id=(up, d), device_id_type=MESH)

    @pl.when(has_down)
    def _():
        pl.semaphore_signal(barrier, inc=1, device_id=(down, d), device_id_type=MESH)

    pl.semaphore_wait(barrier, 3 + jnp.where(has_up, 1, 0) + jnp.where(has_down, 1, 0))

    def times_w(x):
        return jnp.dot(x, w_v[...], preferred_element_type=jnp.float32)

    def times_wt(x):
        return lax.dot_general(
            x, w_v[...], (((1,), (1,)), ((), ())), preferred_element_type=jnp.float32
        )

    def own_chunk(i):
        return rows_at(own + i * chunk, chunk)

    def send_up(src, i):
        @pl.when(has_up)
        def _():
            copy(src.at[own_chunk(i)], uin.at[own_chunk(i)], IDS["up", i], IDS["up", i], up, d).start()

        @pl.when(is_top)
        def _():
            copy(
                src.at[own_chunk(i)], din.at[pl.ds(i * chunk, chunk)],
                IDS["up", i], IDS["down", i], mirror, d,
            ).start()

    def send_up_rest(src):
        @pl.when(has_up)
        def _():
            r = rows_at(rest, quarter)
            copy(src.at[r], uin.at[r], IDS["up_rest"], IDS["up_rest"], up, d).start()

    def send_down(src, i):
        @pl.when(has_down)
        def _():
            copy(
                src.at[own_chunk(i)], din.at[pl.ds(i * chunk, chunk)],
                IDS["down", i], IDS["down", i], down, d,
            ).start()

    def send_x1(src, i):
        copy(src, x1.at[pl.ds(i * chunk, chunk)], IDS["x1", i], IDS["x1", i], mirror, d).start()

    def send_x2(src, i):
        copy(src, arr.at[own_chunk(i)], IDS["x2", i], IDS["x2", i], mirror, d).start()

    def back_even(r):
        prod = times_wt(h_v[r, :])
        dx1[r, :] = (g_v[r, :].astype(jnp.float32) + prod).astype(jnp.bfloat16)

    def back_odd(r):
        dx1[r, :] = times_wt(g_v[r, :]).astype(jnp.bfloat16)

    def forward_odd(r):
        y1[r, :] = (times_w(a_v[r, :]) + h_v[r, :].astype(jnp.float32)).astype(jnp.bfloat16)

    @pl.when(is_even)
    def _():
        for i in range(CHUNKS):
            send_up(a_hbm.at[0], i)
        w_load.wait()
        a_load.wait()

        @pl.loop(0, 1)
        def _(_i):
            s1[...] = times_w(a_v[rows_at(own, quarter), :]).astype(jnp.bfloat16)

        for i in range(CHUNKS):
            send_x1(s1.at[pl.ds(i * chunk, chunk)], i)
        g_load.wait()
        h_load.wait()
        back_even(rows_at(own, quarter))
        for i in range(CHUNKS):
            send_down(dx1, i)
        send_up_rest(a_hbm.at[0])

        pltpu.make_async_copy(a_v, out_hbm.at[0, 0], out_sem.at[0]).start()

        @pl.loop(1, 4)
        def _(k):
            back_even(rows_at(lax.rem(own + k * quarter, rows), quarter))

    @pl.when(is_odd)
    def _():
        for i in range(CHUNKS):
            send_x1(g_hbm.at[0].at[own_chunk(i)], i)
        w_load.wait()
        a_load.wait()
        g_load.wait()
        back_odd(rows_at(own, quarter))
        for i in range(CHUNKS):
            send_up(dx1, i)
        h_load.wait()
        forward_odd(rows_at(own, quarter))
        for i in range(CHUNKS):
            send_down(y1, i)

        @pl.loop(1, 4)
        def _(k):
            back_odd(rows_at(lax.rem(own + k * quarter, rows), quarter))

        send_up_rest(dx1)

        @pl.loop(1, 4)
        def _(k):
            forward_odd(rows_at(lax.rem(own + k * quarter, rows), quarter))

        pltpu.make_async_copy(y1, out_hbm.at[0, 0], out_sem.at[0]).start()

    pltpu.make_async_copy(dx1, grad_hbm.at[0, 0], out_sem.at[1]).start()

    @pl.when(is_bottom)
    def _():
        nb_load.wait()

    for i in range(CHUNKS):
        r, rc = own_chunk(i), pl.ds(i * chunk, chunk)

        @pl.when(has_down)
        def _():
            landed(uin.at[r], ("up", i))
            copy(
                uin.at[r], uin.at[r], IDS["core_up", i], IDS["core_up", i], p, core_peer
            ).start()

        @pl.when(is_even)
        def _():
            s2[rc, :] = times_w(uin[r, :]).astype(jnp.bfloat16)
            send_x2(s2.at[rc], i)

        @pl.when(is_odd)
        def _():
            send_x2(uin.at[r], i)

        landed(din.at[rc], ("down", i))
        landed(x1.at[rc], ("x1", i))

        @pl.when(is_even)
        def _():
            prod = times_wt(x1[rc, :])
            fin[r, :] = (din[rc, :].astype(jnp.float32) + prod).astype(jnp.bfloat16)

        @pl.when(is_odd)
        def _():
            prod = times_w(din[rc, :])
            fin[r, :] = (prod + x1[rc, :].astype(jnp.float32)).astype(jnp.bfloat16)

        copy(fin.at[r], fin.at[r], IDS["fy", i], IDS["fy", i], p, y_peer).start()
        copy(fin.at[r], fin.at[r], IDS["fc", i], IDS["fc", i], p, core_peer).start()

    def y_chunk(i):
        return rows_at(y_own + i * chunk, chunk)

    def pass_on(buf, got, key, i):
        r = y_chunk(i)
        landed(buf.at[r], (got, i))
        copy(buf.at[r], buf.at[r], IDS[key, i], IDS[key, i], p, core_peer).start()

    for i in range(CHUNKS):
        pass_on(fin, "fy", "ff", i)
        r = own_chunk(i)
        landed(arr.at[r], ("x2", i))
        copy(arr.at[r], arr.at[r], IDS["ay", i], IDS["ay", i], p, y_peer).start()
        copy(arr.at[r], arr.at[r], IDS["ac", i], IDS["ac", i], p, core_peer).start()

    @pl.when(has_down)
    def _():
        r = rows_at(rest, quarter)
        landed(uin.at[r], "up_rest")
        copy(uin.at[r], uin.at[r], IDS["core_rest"], IDS["core_rest"], p, core_peer).start()

    def joined_odd(r):
        dx2[r, :] = times_wt(uin[r, :]).astype(jnp.bfloat16)

    @pl.when(is_odd)
    def _():
        @pl.loop(0, 2)
        def _(k):
            joined_odd(rows_at(core * half + k * quarter, quarter))

    for i in range(CHUNKS):
        pass_on(arr, "ay", "af", i)

    @pl.when(has_down)
    def _():
        for i in range(CHUNKS):
            landed(uin.at[rows_at(across + yy * quarter + i * chunk, chunk)], ("core_up", i))
        landed(uin.at[rows_at(across + (1 - yy) * quarter, quarter)], "core_rest")

    @pl.when(is_odd)
    def _():
        @pl.loop(0, 2)
        def _(k):
            joined_odd(rows_at(across + k * quarter, quarter))

    for i in range(CHUNKS):
        landed(fin.at[rows_at(across + yy * quarter + i * chunk, chunk)], ("fc", i))
        landed(fin.at[rows_at(across + (1 - yy) * quarter + i * chunk, chunk)], ("ff", i))

    @pl.when(is_even)
    def _():
        pltpu.make_async_copy(uin, out_hbm.at[0, 1], out_sem.at[2]).start()
        pltpu.make_async_copy(fin, grad_hbm.at[0, 1], out_sem.at[3]).start()

    @pl.when(is_odd)
    def _():
        pltpu.make_async_copy(dx2, grad_hbm.at[0, 1], out_sem.at[2]).start()
        pltpu.make_async_copy(fin, out_hbm.at[0, 1], out_sem.at[3]).start()

    for i in range(CHUNKS):
        landed(arr.at[rows_at(across + yy * quarter + i * chunk, chunk)], ("ac", i))
        landed(arr.at[rows_at(across + (1 - yy) * quarter + i * chunk, chunk)], ("af", i))
    pltpu.make_async_copy(arr, arr_hbm.at[0], out_sem.at[4]).start()

    piece = x1.at[pl.ds(0, chunk)]
    for i in range(CHUNKS):
        for kind in ("up", "x1", "x2", "fc", "fy", "ff", "ac", "ay", "af"):
            sent(piece, (kind, i))

    @pl.when(has_up)
    def _():
        sent(x1, "up_rest")

    @pl.when(has_down)
    def _():
        for i in range(CHUNKS):
            sent(piece, ("down", i))
            sent(piece, ("core_up", i))
        sent(x1, "core_rest")

    for i in range(5):
        pltpu.make_async_copy(arr, arr_hbm.at[0], out_sem.at[i]).wait()


def local(count, a, h, g, nb, lc, w):
    _, rows, width = a.shape
    bf16 = jnp.bfloat16
    full = pltpu.VMEM((rows, width), bf16)
    quarter = pltpu.VMEM((rows // 4, width), bf16)
    anywhere = pl.BlockSpec(memory_space=pl.ANY)
    return pl.pallas_call(
        functools.partial(kernel, count),
        out_shape=(
            jax.ShapeDtypeStruct((1, 2, rows, width), bf16),
            jax.ShapeDtypeStruct((1, 2, rows, width), bf16),
            jax.ShapeDtypeStruct((1, rows, width), bf16),
        ),
        in_specs=[anywhere] * 6,
        out_specs=(anywhere,) * 3,
        scratch_shapes=[
            full, full, full, pltpu.VMEM((width, width), bf16),
            full, quarter, quarter, full, full, full, full, full, quarter, quarter,
            pltpu.SemaphoreType.DMA((5,)),
            pltpu.SemaphoreType.DMA((5,)),
            pltpu.SemaphoreType.DMA((len(IDS),)),
            pltpu.SemaphoreType.DMA((len(IDS),)),
        ],
        compiler_params=pltpu.CompilerParams(
            collective_id=0, has_side_effects=True, vmem_limit_bytes=48 * 1024 * 1024
        ),
        cost_estimate=pl.CostEstimate(
            flops=8 * rows * width * width,
            bytes_accessed=16 * rows * width + 2 * width * width,
            transcendentals=0,
        ),
    )(a, h, g, nb, lc, w)


def solution(mesh):
    in_specs = (
        P("section", None, None),
        P("section", None, None),
        P("section", None, None),
        P(),
        P(),
        P("section", None, None),
    )
    out_specs = (
        P(("dp", "section"), None, None, None),
        P(("dp", "section"), None, None, None),
        P(("dp", "section"), None, None),
    )
    return jax.shard_map(
        functools.partial(local, mesh.shape["section"]),
        mesh=mesh, in_specs=in_specs, out_specs=out_specs, check_vma=False,
    )
```

```python
import functools

import jax
import jax.numpy as jnp
from jax import lax
from jax.experimental import pallas as pl
from jax.experimental.pallas import tpu as pltpu
from jax.sharding import PartitionSpec as P

MESH = pl.DeviceIdType.MESH
CHUNKS = 3


def message_ids():
    ids = {}
    for kind in ("up", "down", "x1", "x2", "core_up", "fc", "fy", "ff", "ac", "ay", "af"):
        for i in range(CHUNKS):
            ids[kind, i] = len(ids)
    for kind in ("up_rest", "core_rest"):
        ids[kind] = len(ids)
    return ids


IDS = message_ids()


def kernel(
    count,
    a_hbm, h_hbm, g_hbm, nb_hbm, lc_hbm, w_hbm,
    y1, dx1, uin, dx2, fin, arr,
    a_v, h_v, g_v, w_v, din, x1, s1, s2,
    in_sem, send_sem, recv_sem,
):
    rows, _ = a_v.shape
    half, quarter = rows // 2, rows // 4
    chunk = quarter // CHUNKS
    p = lax.axis_index("section")
    d = lax.axis_index("dp")
    mirror = p + 1 - 2 * (p % 2)
    core_peer = d + 1 - 2 * (d % 2)
    y_peer = d + 2 - 4 * ((d // 2) % 2)
    core, yy = d % 2, (d // 2) % 2
    is_even = p % 2 == 0
    is_odd = p % 2 == 1
    has_up = p + 2 < count
    is_top = p + 2 >= count
    has_down = p >= 2
    is_bottom = p < 2
    up = jnp.where(has_up, p + 2, p)
    down = jnp.where(has_down, p - 2, p)

    own = core * half + yy * quarter
    rest = core * half + (1 - yy) * quarter
    across = (1 - core) * half
    y_own = rest

    def rows_at(start, size):
        return pl.ds(pl.multiple_of(start, 16), size)

    def copy(src, dst, ks, kr, section, dp):
        return pltpu.make_async_remote_copy(
            src_ref=src, dst_ref=dst, send_sem=send_sem.at[ks], recv_sem=recv_sem.at[kr],
            device_id=(section, dp), device_id_type=MESH,
        )

    def landed(dst, key):
        k = IDS[key]
        copy(dst, dst, k, k, mirror, d).wait_recv()

    def sent(src, key):
        k = IDS[key]
        copy(src, src, k, k, mirror, d).wait_send()

    loads = [
        pltpu.make_async_copy(src, dst, in_sem.at[i])
        for i, (src, dst) in enumerate(
            ((w_hbm.at[0], w_v), (a_hbm.at[0], a_v), (g_hbm.at[0], g_v), (h_hbm.at[0], h_v))
        )
    ]
    w_load, a_load, g_load, h_load = loads
    for load in loads:
        load.start()
    nb_load = pltpu.make_async_copy(nb_hbm, uin, in_sem.at[4])
    lc_load = pltpu.make_async_copy(lc_hbm, uin, in_sem.at[4])
    y1_load = pltpu.make_async_copy(a_hbm.at[0], y1, in_sem.at[5])

    @pl.when(p == 0)
    def _():
        nb_load.start()

    @pl.when(p == 1)
    def _():
        lc_load.start()

    barrier = pltpu.get_barrier_semaphore()
    for peer in ((mirror, d), (p, core_peer), (p, y_peer)):
        pl.semaphore_signal(barrier, inc=1, device_id=peer, device_id_type=MESH)

    @pl.when(has_up)
    def _():
        pl.semaphore_signal(barrier, inc=1, device_id=(up, d), device_id_type=MESH)

    @pl.when(has_down)
    def _():
        pl.semaphore_signal(barrier, inc=1, device_id=(down, d), device_id_type=MESH)

    pl.semaphore_wait(barrier, 3 + jnp.where(has_up, 1, 0) + jnp.where(has_down, 1, 0))

    def times_w(x):
        return jnp.dot(x, w_v[...], preferred_element_type=jnp.float32)

    def times_wt(x):
        return lax.dot_general(
            x, w_v[...], (((1,), (1,)), ((), ())), preferred_element_type=jnp.float32
        )

    def own_chunk(i):
        return rows_at(own + i * chunk, chunk)

    def send_up(src, i):
        @pl.when(has_up)
        def _():
            copy(src.at[own_chunk(i)], uin.at[own_chunk(i)], IDS["up", i], IDS["up", i], up, d).start()

        @pl.when(is_top)
        def _():
            copy(
                src.at[own_chunk(i)], din.at[pl.ds(i * chunk, chunk)],
                IDS["up", i], IDS["down", i], mirror, d,
            ).start()

    def send_up_rest(src):
        @pl.when(has_up)
        def _():
            r = rows_at(rest, quarter)
            copy(src.at[r], uin.at[r], IDS["up_rest"], IDS["up_rest"], up, d).start()

    def send_down(src, i):
        @pl.when(has_down)
        def _():
            copy(
                src.at[own_chunk(i)], din.at[pl.ds(i * chunk, chunk)],
                IDS["down", i], IDS["down", i], down, d,
            ).start()

    def send_x1(src, i):
        copy(src, x1.at[pl.ds(i * chunk, chunk)], IDS["x1", i], IDS["x1", i], mirror, d).start()

    def send_x2(src, i):
        copy(src, arr.at[own_chunk(i)], IDS["x2", i], IDS["x2", i], mirror, d).start()

    def back_even(r):
        prod = times_wt(h_v[r, :])
        dx1[r, :] = (g_v[r, :].astype(jnp.float32) + prod).astype(jnp.bfloat16)

    def back_odd(r):
        dx1[r, :] = times_wt(g_v[r, :]).astype(jnp.bfloat16)

    def forward_odd(r):
        y1[r, :] = (times_w(a_v[r, :]) + h_v[r, :].astype(jnp.float32)).astype(jnp.bfloat16)

    def part(k):
        return rows_at(lax.rem(own + k * quarter, rows), quarter)

    @pl.when(is_even)
    def _():
        send_up(a_hbm.at[0], 0)
        w_load.wait()
        a_load.wait()
        s1[...] = times_w(a_v[rows_at(own, quarter), :]).astype(jnp.bfloat16)
        send_x1(s1.at[pl.ds(0, chunk)], 0)
        g_load.wait()
        h_load.wait()
        back_even(part(0))
        send_down(dx1, 0)
        y1_load.start()

    @pl.when(is_odd)
    def _():
        send_x1(g_hbm.at[0].at[own_chunk(0)], 0)
        w_load.wait()
        a_load.wait()
        g_load.wait()
        back_odd(part(0))
        send_up(dx1, 0)
        h_load.wait()
        forward_odd(part(0))
        send_down(y1, 0)

    @pl.when(is_bottom)
    def _():
        nb_load.wait()

    def y_chunk(i):
        return rows_at(y_own + i * chunk, chunk)

    def pass_on(buf, got, key, i):
        r = y_chunk(i)
        landed(buf.at[r], (got, i))
        copy(buf.at[r], buf.at[r], IDS[key, i], IDS[key, i], p, core_peer).start()

    piece = x1.at[pl.ds(0, chunk)]
    for i in range(CHUNKS + 1):
        if i < CHUNKS:
            r, rc = own_chunk(i), pl.ds(i * chunk, chunk)

            @pl.when(is_even)
            def _():
                if i < 3:
                    back_even(part(i + 1))

            @pl.when(is_odd)
            def _():
                if i < 3:
                    back_odd(part(i + 1))
                    forward_odd(part(i + 1))

            sent(piece, ("x1", i))
            if i + 1 < CHUNKS:
                @pl.when(is_even)
                def _():
                    send_x1(s1.at[pl.ds((i + 1) * chunk, chunk)], i + 1)

                @pl.when(is_odd)
                def _():
                    send_x1(g_hbm.at[0].at[own_chunk(i + 1)], i + 1)

            sent(piece, ("up", i))

            @pl.when(is_even)
            def _():
                if i + 1 < CHUNKS:
                    send_up(a_hbm.at[0], i + 1)
                else:
                    send_up_rest(a_hbm.at[0])

            @pl.when(is_odd)
            def _():
                if i + 1 < CHUNKS:
                    send_up(dx1, i + 1)
                else:
                    send_up_rest(dx1)

            @pl.when(has_down)
            def _():
                sent(piece, ("down", i))
                if i + 1 < CHUNKS:
                    @pl.when(is_even)
                    def _():
                        send_down(dx1, i + 1)

                    @pl.when(is_odd)
                    def _():
                        send_down(y1, i + 1)

            @pl.when(has_down)
            def _():
                landed(uin.at[r], ("up", i))
                k = IDS["core_up", i]
                copy(uin.at[r], uin.at[r], k, k, p, core_peer).start()

            @pl.when(is_even)
            def _():
                s2[rc, :] = times_w(uin[r, :]).astype(jnp.bfloat16)
                send_x2(s2.at[rc], i)

            @pl.when(is_odd)
            def _():
                send_x2(uin.at[r], i)

            landed(din.at[rc], ("down", i))
            landed(x1.at[rc], ("x1", i))

            @pl.when(is_even)
            def _():
                prod = times_wt(x1[rc, :])
                fin[r, :] = (din[rc, :].astype(jnp.float32) + prod).astype(jnp.bfloat16)

            @pl.when(is_odd)
            def _():
                prod = times_w(din[rc, :])
                fin[r, :] = (prod + x1[rc, :].astype(jnp.float32)).astype(jnp.bfloat16)

            copy(fin.at[r], fin.at[r], IDS["fy", i], IDS["fy", i], p, y_peer).start()
            copy(fin.at[r], fin.at[r], IDS["fc", i], IDS["fc", i], p, core_peer).start()
        if i > 0:
            r = own_chunk(i - 1)
            landed(arr.at[r], ("x2", i - 1))
            k = IDS["ay", i - 1]
            copy(arr.at[r], arr.at[r], k, k, p, y_peer).start()
            k = IDS["ac", i - 1]
            copy(arr.at[r], arr.at[r], k, k, p, core_peer).start()
            pass_on(fin, "fy", "ff", i - 1)

    @pl.when(has_down)
    def _():
        r = rows_at(rest, quarter)
        landed(uin.at[r], "up_rest")
        copy(uin.at[r], uin.at[r], IDS["core_rest"], IDS["core_rest"], p, core_peer).start()

    def joined_odd(r):
        dx2[r, :] = times_wt(uin[r, :]).astype(jnp.bfloat16)

    @pl.when(is_odd)
    def _():
        @pl.loop(0, 2)
        def _(k):
            joined_odd(rows_at(core * half + k * quarter, quarter))

    for i in range(CHUNKS - 1):
        pass_on(arr, "ay", "af", i)

    @pl.when(has_down)
    def _():
        for i in range(CHUNKS):
            landed(uin.at[rows_at(across + yy * quarter + i * chunk, chunk)], ("core_up", i))
        landed(uin.at[rows_at(across + (1 - yy) * quarter, quarter)], "core_rest")

    @pl.when(is_odd)
    def _():
        @pl.loop(0, 2)
        def _(k):
            joined_odd(rows_at(across + k * quarter, quarter))

    pass_on(arr, "ay", "af", CHUNKS - 1)
    for i in range(CHUNKS):
        landed(fin.at[rows_at(across + yy * quarter + i * chunk, chunk)], ("fc", i))
        landed(fin.at[rows_at(across + (1 - yy) * quarter + i * chunk, chunk)], ("ff", i))
    for i in range(CHUNKS):
        landed(arr.at[rows_at(across + yy * quarter + i * chunk, chunk)], ("ac", i))
        landed(arr.at[rows_at(across + (1 - yy) * quarter + i * chunk, chunk)], ("af", i))

    @pl.when(is_even)
    def _():
        y1_load.wait()

    for i in range(CHUNKS):
        for kind in ("x2", "fc", "fy", "ff", "ac", "ay", "af"):
            sent(piece, (kind, i))

    @pl.when(has_up)
    def _():
        sent(x1, "up_rest")

    @pl.when(has_down)
    def _():
        for i in range(CHUNKS):
            sent(piece, ("core_up", i))
        sent(x1, "core_rest")


def write_out(y1, dx1, uin, dx2, fin, arr, out_hbm, grad_hbm, arr_hbm, sem):
    is_even = lax.axis_index("section") % 2 == 0
    pltpu.make_async_copy(y1, out_hbm.at[0, 0], sem.at[0]).start()
    pltpu.make_async_copy(dx1, grad_hbm.at[0, 0], sem.at[1]).start()
    pltpu.make_async_copy(arr, arr_hbm.at[0], sem.at[2]).start()

    @pl.when(is_even)
    def _():
        pltpu.make_async_copy(uin, out_hbm.at[0, 1], sem.at[3]).start()
        pltpu.make_async_copy(fin, grad_hbm.at[0, 1], sem.at[4]).start()

    @pl.when(jnp.logical_not(is_even))
    def _():
        pltpu.make_async_copy(dx2, grad_hbm.at[0, 1], sem.at[3]).start()
        pltpu.make_async_copy(fin, out_hbm.at[0, 1], sem.at[4]).start()

    for i in range(5):
        pltpu.make_async_copy(arr, arr_hbm.at[0], sem.at[i]).wait()


def local(count, a, h, g, nb, lc, w):
    _, rows, width = a.shape
    bf16 = jnp.bfloat16
    full = pltpu.VMEM((rows, width), bf16)
    quarter = pltpu.VMEM((rows // 4, width), bf16)
    results = pl.pallas_call(
        functools.partial(kernel, count),
        out_shape=(full,) * 6,
        in_specs=[pl.BlockSpec(memory_space=pltpu.HBM)] * 6,
        out_specs=(pl.BlockSpec(memory_space=pltpu.VMEM),) * 6,
        scratch_shapes=[
            full, full, full, pltpu.VMEM((width, width), bf16),
            quarter, quarter, quarter, quarter,
            pltpu.SemaphoreType.DMA((6,)),
            pltpu.SemaphoreType.DMA((len(IDS),)),
            pltpu.SemaphoreType.DMA((len(IDS),)),
        ],
        compiler_params=pltpu.CompilerParams(
            collective_id=0, has_side_effects=True, vmem_limit_bytes=52 * 1024 * 1024
        ),
        cost_estimate=pl.CostEstimate(
            flops=8 * rows * width * width,
            bytes_accessed=6 * rows * width + 2 * width * width,
            transcendentals=0,
        ),
    )(a, h, g, nb, lc, w)
    return pl.pallas_call(
        write_out,
        out_shape=(
            jax.ShapeDtypeStruct((1, 2, rows, width), bf16),
            jax.ShapeDtypeStruct((1, 2, rows, width), bf16),
            jax.ShapeDtypeStruct((1, rows, width), bf16),
        ),
        in_specs=[pl.BlockSpec(memory_space=pl.ANY)] * 6,
        out_specs=(pl.BlockSpec(memory_space=pltpu.HBM),) * 3,
        scratch_shapes=[pltpu.SemaphoreType.DMA((5,))],
        compiler_params=pltpu.CompilerParams(vmem_limit_bytes=1024 * 1024),
        cost_estimate=pl.CostEstimate(
            flops=0, bytes_accessed=10 * rows * width, transcendentals=0
        ),
    )(*results)


def solution(mesh):
    in_specs = (
        P("section", None, None),
        P("section", None, None),
        P("section", None, None),
        P(),
        P(),
        P("section", None, None),
    )
    out_specs = (
        P(("dp", "section"), None, None, None),
        P(("dp", "section"), None, None, None),
        P(("dp", "section"), None, None),
    )
    return jax.shard_map(
        functools.partial(local, mesh.shape["section"]),
        mesh=mesh, in_specs=in_specs, out_specs=out_specs, check_vma=False,
    )
```

```python
import functools

import jax
import jax.numpy as jnp
from jax import lax
from jax.experimental import pallas as pl
from jax.experimental.pallas import tpu as pltpu
from jax.sharding import PartitionSpec as P

MESH = pl.DeviceIdType.MESH
CHUNKS = 4
AHEAD = 2


def message_ids():
    ids = {}
    for kind in ("up", "down", "x1", "x2", "core_up", "fc", "fy", "ff", "ac", "ay", "af"):
        for i in range(CHUNKS):
            ids[kind, i] = len(ids)
    for kind in ("up_rest", "core_rest"):
        ids[kind] = len(ids)
    return ids


IDS = message_ids()


def kernel(
    count,
    a_hbm, h_hbm, g_hbm, nb_hbm, lc_hbm, w_hbm,
    y1, dx1, uin, dx2, fin, arr,
    a_v, h_v, g_v, w_v, din, x1, s1, s2,
    in_sem, send_sem, recv_sem,
):
    rows, _ = a_v.shape
    half, quarter = rows // 2, rows // 4
    chunk = quarter // CHUNKS
    p = lax.axis_index("section")
    d = lax.axis_index("dp")
    mirror = p + 1 - 2 * (p % 2)
    core_peer = d + 1 - 2 * (d % 2)
    y_peer = d + 2 - 4 * ((d // 2) % 2)
    core, yy = d % 2, (d // 2) % 2
    is_even = p % 2 == 0
    is_odd = p % 2 == 1
    has_up = p + 2 < count
    is_top = p + 2 >= count
    has_down = p >= 2
    is_bottom = p < 2
    up = jnp.where(has_up, p + 2, p)
    down = jnp.where(has_down, p - 2, p)

    own = core * half + yy * quarter
    rest = core * half + (1 - yy) * quarter
    across = (1 - core) * half
    y_own = rest

    def rows_at(start, size):
        return pl.ds(pl.multiple_of(start, 16), size)

    def copy(src, dst, ks, kr, section, dp):
        return pltpu.make_async_remote_copy(
            src_ref=src, dst_ref=dst, send_sem=send_sem.at[ks], recv_sem=recv_sem.at[kr],
            device_id=(section, dp), device_id_type=MESH,
        )

    def landed(dst, key):
        k = IDS[key]
        copy(dst, dst, k, k, mirror, d).wait_recv()

    def sent(src, key):
        k = IDS[key]
        copy(src, src, k, k, mirror, d).wait_send()

    loads = [
        pltpu.make_async_copy(src, dst, in_sem.at[i])
        for i, (src, dst) in enumerate(
            ((w_hbm.at[0], w_v), (a_hbm.at[0], a_v), (g_hbm.at[0], g_v), (h_hbm.at[0], h_v))
        )
    ]
    w_load, a_load, g_load, h_load = loads
    for load in loads:
        load.start()
    nb_load = pltpu.make_async_copy(nb_hbm, uin, in_sem.at[4])
    lc_load = pltpu.make_async_copy(lc_hbm, uin, in_sem.at[4])
    y1_load = pltpu.make_async_copy(a_hbm.at[0], y1, in_sem.at[5])

    @pl.when(p == 0)
    def _():
        nb_load.start()

    @pl.when(p == 1)
    def _():
        lc_load.start()

    barrier = pltpu.get_barrier_semaphore()
    for peer in ((mirror, d), (p, core_peer), (p, y_peer)):
        pl.semaphore_signal(barrier, inc=1, device_id=peer, device_id_type=MESH)

    @pl.when(has_up)
    def _():
        pl.semaphore_signal(barrier, inc=1, device_id=(up, d), device_id_type=MESH)

    @pl.when(has_down)
    def _():
        pl.semaphore_signal(barrier, inc=1, device_id=(down, d), device_id_type=MESH)

    pl.semaphore_wait(barrier, 3 + jnp.where(has_up, 1, 0) + jnp.where(has_down, 1, 0))

    def times_w(x):
        return jnp.dot(x, w_v[...], preferred_element_type=jnp.float32)

    def times_wt(x):
        return lax.dot_general(
            x, w_v[...], (((1,), (1,)), ((), ())), preferred_element_type=jnp.float32
        )

    def own_chunk(i):
        return rows_at(own + i * chunk, chunk)

    def send_up(src, i):
        @pl.when(has_up)
        def _():
            copy(src.at[own_chunk(i)], uin.at[own_chunk(i)], IDS["up", i], IDS["up", i], up, d).start()

        @pl.when(is_top)
        def _():
            copy(
                src.at[own_chunk(i)], din.at[pl.ds(i * chunk, chunk)],
                IDS["up", i], IDS["down", i], mirror, d,
            ).start()

    def send_up_rest(src):
        @pl.when(has_up)
        def _():
            r = rows_at(rest, quarter)
            copy(src.at[r], uin.at[r], IDS["up_rest"], IDS["up_rest"], up, d).start()

    def send_down(src, i):
        @pl.when(has_down)
        def _():
            copy(
                src.at[own_chunk(i)], din.at[pl.ds(i * chunk, chunk)],
                IDS["down", i], IDS["down", i], down, d,
            ).start()

    def send_x1(src, i):
        copy(src, x1.at[pl.ds(i * chunk, chunk)], IDS["x1", i], IDS["x1", i], mirror, d).start()

    def send_x2(src, i):
        copy(src, arr.at[own_chunk(i)], IDS["x2", i], IDS["x2", i], mirror, d).start()

    def back_even(r):
        prod = times_wt(h_v[r, :])
        dx1[r, :] = (g_v[r, :].astype(jnp.float32) + prod).astype(jnp.bfloat16)

    def back_odd(r):
        dx1[r, :] = times_wt(g_v[r, :]).astype(jnp.bfloat16)

    def forward_odd(r):
        y1[r, :] = (times_w(a_v[r, :]) + h_v[r, :].astype(jnp.float32)).astype(jnp.bfloat16)

    parts = [rows_at(start, quarter) for start in (rest, across, across + quarter)]

    @pl.when(is_even)
    def _():
        for i in range(AHEAD):
            send_up(a_hbm.at[0], i)
        w_load.wait()
        a_load.wait()
        s1[...] = times_w(a_v[rows_at(own, quarter), :]).astype(jnp.bfloat16)
        for i in range(AHEAD):
            send_x1(s1.at[pl.ds(i * chunk, chunk)], i)
        g_load.wait()
        h_load.wait()
        back_even(rows_at(own, quarter))
        for i in range(AHEAD):
            send_down(dx1, i)
        y1_load.start()

    @pl.when(is_odd)
    def _():
        for i in range(AHEAD):
            send_x1(g_hbm.at[0].at[own_chunk(i)], i)
        w_load.wait()
        a_load.wait()
        g_load.wait()
        back_odd(rows_at(own, quarter))
        for i in range(AHEAD):
            send_up(dx1, i)
        h_load.wait()
        forward_odd(rows_at(own, quarter))
        for i in range(AHEAD):
            send_down(y1, i)

    @pl.when(is_bottom)
    def _():
        nb_load.wait()

    def y_chunk(i):
        return rows_at(y_own + i * chunk, chunk)

    def pass_on(buf, got, key, i):
        r = y_chunk(i)
        landed(buf.at[r], (got, i))
        copy(buf.at[r], buf.at[r], IDS[key, i], IDS[key, i], p, core_peer).start()

    def joined_odd(r):
        dx2[r, :] = times_wt(uin[r, :]).astype(jnp.bfloat16)

    piece = x1.at[pl.ds(0, chunk)]
    for i in range(CHUNKS + 1):
        if i < CHUNKS:
            r, rc = own_chunk(i), pl.ds(i * chunk, chunk)

            @pl.when(is_even)
            def _():
                if i < 3:
                    back_even(parts[i])

            @pl.when(is_odd)
            def _():
                if i < 3:
                    back_odd(parts[i])
                    forward_odd(parts[i])

            sent(piece, ("x1", i))
            if i + AHEAD < CHUNKS:
                @pl.when(is_even)
                def _():
                    send_x1(s1.at[pl.ds((i + AHEAD) * chunk, chunk)], i + AHEAD)

                @pl.when(is_odd)
                def _():
                    send_x1(g_hbm.at[0].at[own_chunk(i + AHEAD)], i + AHEAD)

            sent(piece, ("up", i))

            @pl.when(is_even)
            def _():
                if i + AHEAD < CHUNKS:
                    send_up(a_hbm.at[0], i + AHEAD)
                elif i + AHEAD == CHUNKS:
                    send_up_rest(a_hbm.at[0])

            @pl.when(is_odd)
            def _():
                if i + AHEAD < CHUNKS:
                    send_up(dx1, i + AHEAD)
                elif i + AHEAD == CHUNKS:
                    send_up_rest(dx1)

            @pl.when(has_down)
            def _():
                sent(piece, ("down", i))
                if i + AHEAD < CHUNKS:
                    @pl.when(is_even)
                    def _():
                        send_down(dx1, i + AHEAD)

                    @pl.when(is_odd)
                    def _():
                        send_down(y1, i + AHEAD)

            @pl.when(has_down)
            def _():
                landed(uin.at[r], ("up", i))
                k = IDS["core_up", i]
                copy(uin.at[r], uin.at[r], k, k, p, core_peer).start()

            @pl.when(is_even)
            def _():
                s2[rc, :] = times_w(uin[r, :]).astype(jnp.bfloat16)
                send_x2(s2.at[rc], i)

            @pl.when(is_odd)
            def _():
                send_x2(uin.at[r], i)

            landed(din.at[rc], ("down", i))
            landed(x1.at[rc], ("x1", i))

            @pl.when(is_even)
            def _():
                prod = times_wt(x1[rc, :])
                fin[r, :] = (din[rc, :].astype(jnp.float32) + prod).astype(jnp.bfloat16)

            @pl.when(is_odd)
            def _():
                prod = times_w(din[rc, :])
                fin[r, :] = (prod + x1[rc, :].astype(jnp.float32)).astype(jnp.bfloat16)

            copy(fin.at[r], fin.at[r], IDS["fy", i], IDS["fy", i], p, y_peer).start()
            copy(fin.at[r], fin.at[r], IDS["fc", i], IDS["fc", i], p, core_peer).start()
        if i > 0:
            r = own_chunk(i - 1)
            landed(arr.at[r], ("x2", i - 1))
            k = IDS["ay", i - 1]
            copy(arr.at[r], arr.at[r], k, k, p, y_peer).start()
            k = IDS["ac", i - 1]
            copy(arr.at[r], arr.at[r], k, k, p, core_peer).start()
            pass_on(fin, "fy", "ff", i - 1)
        if i == CHUNKS - 1:
            @pl.when(is_odd)
            def _():
                joined_odd(rows_at(own, quarter))

    for i in range(CHUNKS - 2):
        pass_on(arr, "ay", "af", i)

    @pl.when(has_down)
    def _():
        r = rows_at(rest, quarter)
        landed(uin.at[r], "up_rest")
        copy(uin.at[r], uin.at[r], IDS["core_rest"], IDS["core_rest"], p, core_peer).start()
        for i in range(CHUNKS):
            landed(uin.at[rows_at(across + yy * quarter + i * chunk, chunk)], ("core_up", i))

    @pl.when(is_odd)
    def _():
        joined_odd(rows_at(rest, quarter))
        joined_odd(rows_at(across + yy * quarter, quarter))

    pass_on(arr, "ay", "af", CHUNKS - 2)

    @pl.when(has_down)
    def _():
        landed(uin.at[rows_at(across + (1 - yy) * quarter, quarter)], "core_rest")

    @pl.when(is_odd)
    def _():
        joined_odd(rows_at(across + (1 - yy) * quarter, quarter))

    pass_on(arr, "ay", "af", CHUNKS - 1)
    for i in range(CHUNKS):
        landed(fin.at[rows_at(across + yy * quarter + i * chunk, chunk)], ("fc", i))
        landed(fin.at[rows_at(across + (1 - yy) * quarter + i * chunk, chunk)], ("ff", i))
    for i in range(CHUNKS):
        landed(arr.at[rows_at(across + yy * quarter + i * chunk, chunk)], ("ac", i))
        landed(arr.at[rows_at(across + (1 - yy) * quarter + i * chunk, chunk)], ("af", i))

    @pl.when(is_even)
    def _():
        y1_load.wait()

    for i in range(CHUNKS):
        for kind in ("x2", "fc", "fy", "ff", "ac", "ay", "af"):
            sent(piece, (kind, i))

    @pl.when(has_up)
    def _():
        sent(x1, "up_rest")

    @pl.when(has_down)
    def _():
        for i in range(CHUNKS):
            sent(piece, ("core_up", i))
        sent(x1, "core_rest")


def write_out(y1, dx1, uin, dx2, fin, arr, out_hbm, grad_hbm, arr_hbm, sem):
    is_even = lax.axis_index("section") % 2 == 0
    pltpu.make_async_copy(y1, out_hbm.at[0, 0], sem.at[0]).start()
    pltpu.make_async_copy(dx1, grad_hbm.at[0, 0], sem.at[1]).start()
    pltpu.make_async_copy(arr, arr_hbm.at[0], sem.at[2]).start()

    @pl.when(is_even)
    def _():
        pltpu.make_async_copy(uin, out_hbm.at[0, 1], sem.at[3]).start()
        pltpu.make_async_copy(fin, grad_hbm.at[0, 1], sem.at[4]).start()

    @pl.when(jnp.logical_not(is_even))
    def _():
        pltpu.make_async_copy(dx2, grad_hbm.at[0, 1], sem.at[3]).start()
        pltpu.make_async_copy(fin, out_hbm.at[0, 1], sem.at[4]).start()

    for i in range(5):
        pltpu.make_async_copy(arr, arr_hbm.at[0], sem.at[i]).wait()


def local(count, a, h, g, nb, lc, w):
    _, rows, width = a.shape
    bf16 = jnp.bfloat16
    full = pltpu.VMEM((rows, width), bf16)
    quarter = pltpu.VMEM((rows // 4, width), bf16)
    results = pl.pallas_call(
        functools.partial(kernel, count),
        out_shape=(full,) * 6,
        in_specs=[pl.BlockSpec(memory_space=pltpu.HBM)] * 6,
        out_specs=(pl.BlockSpec(memory_space=pltpu.VMEM),) * 6,
        scratch_shapes=[
            full, full, full, pltpu.VMEM((width, width), bf16),
            quarter, quarter, quarter, quarter,
            pltpu.SemaphoreType.DMA((6,)),
            pltpu.SemaphoreType.DMA((len(IDS),)),
            pltpu.SemaphoreType.DMA((len(IDS),)),
        ],
        compiler_params=pltpu.CompilerParams(
            collective_id=0, has_side_effects=True, vmem_limit_bytes=52 * 1024 * 1024
        ),
        cost_estimate=pl.CostEstimate(
            flops=8 * rows * width * width,
            bytes_accessed=6 * rows * width + 2 * width * width,
            transcendentals=0,
        ),
    )(a, h, g, nb, lc, w)
    return pl.pallas_call(
        write_out,
        out_shape=(
            jax.ShapeDtypeStruct((1, 2, rows, width), bf16),
            jax.ShapeDtypeStruct((1, 2, rows, width), bf16),
            jax.ShapeDtypeStruct((1, rows, width), bf16),
        ),
        in_specs=[pl.BlockSpec(memory_space=pl.ANY)] * 6,
        out_specs=(pl.BlockSpec(memory_space=pltpu.HBM),) * 3,
        scratch_shapes=[pltpu.SemaphoreType.DMA((5,))],
        compiler_params=pltpu.CompilerParams(vmem_limit_bytes=1024 * 1024),
        cost_estimate=pl.CostEstimate(
            flops=0, bytes_accessed=10 * rows * width, transcendentals=0
        ),
    )(*results)


def solution(mesh):
    in_specs = (
        P("section", None, None),
        P("section", None, None),
        P("section", None, None),
        P(),
        P(),
        P("section", None, None),
    )
    out_specs = (
        P(("dp", "section"), None, None, None),
        P(("dp", "section"), None, None, None),
        P(("dp", "section"), None, None),
    )
    return jax.shard_map(
        functools.partial(local, mesh.shape["section"]),
        mesh=mesh, in_specs=in_specs, out_specs=out_specs, check_vma=False,
    )
```
